32 devices in a mesh: dom: 8 (over z, x), feat: 4 (over y, core).
Axes of the slice: x: 2, y: 2, z: 4, core: 2. Of those that a mesh axis runs over, the one named last changes fastest.
Arguments:
- feats: bfloat16 [16384, 768], P('dom', 'feat'), may hold values from -6 to 6
- tile_vals: bfloat16 [1536, 128, 128], P('dom'), may hold values from 0 to 1
- tile_dst: int32 [1536], P('dom'), may hold values from 0 to 15
- tile_src: int32 [1536], P('dom'), may hold values from 0 to 79
- tile_count: int32 [8], P('dom'), may hold values from 96 to 192, as said below
- send_blocks: int32 [8, 8, 8], P('dom'), may hold values from 0 to 15
- send_count: int32 [8, 8], P('dom'), may hold values from 1 to 8, as said below
- w_self: bfloat16 [3, 768, 768], replicated, may hold values from -0.21875 to 0.21875
- w_nbr: bfloat16 [3, 768, 768], replicated, may hold values from -0.21875 to 0.21875
- bias: float32 [3, 768], replicated, may hold values from -3 to 3
Outputs:
- hidden: bfloat16 [16384, 768], P('dom', 'feat')
The draws below stay inside these ranges and needn't reach their ends.
Inputs may be any that keep to these rules, and one draw needn't show every extreme that they name: `tile_count`: some partition has exactly 192 live tiles. `send_count`: some partition sends exactly 8 blocks to some peer.
All inputs are finite; a program needn't handle non-finite values.
Results may differ from the reference program's by a relative error of at most 0.0085.
Values may be sent and summed in bfloat16 or wider, within the bound.
No kernel may reach another device: no remote copies, remote signals or barrier semaphores. Data moves between devices by JAX's collectives and lax.ppermute only.
A program may use at most 128 MiB of HBM per device.

```python
import jax
import jax.numpy as jnp
from jax import lax

D = 768
LAYERS = 3
BLK = 128
PEERS = 8
NODE_DEV = 2048
TILES_DEV = 192
SLOTS = 8
BLK_DEV = 16
NODES = 16384
TILES = 1536
SRCS = 80
N_DOM = 8


def draw_tile_vals(key, part):
    first, second, third = jax.random.split(jax.random.fold_in(key, 11), 3)
    picks = jax.random.uniform(first, (TILES, BLK, BLK), jnp.float32)
    present = (picks < 3.0 / BLK).astype(jnp.float32)
    diag_mask = jnp.eye(BLK, dtype=jnp.float32)[None, :, :]
    entries = jax.random.uniform(second, (TILES, BLK, BLK), jnp.float32, 0.25, 1.0)
    diag_vals = jax.random.uniform(third, (TILES, BLK, BLK), jnp.float32, 0.5, 1.0)
    off_part = entries * present * (1.0 - diag_mask)
    return (off_part + diag_vals * diag_mask).astype(jnp.bfloat16)


def draw_tile_count(key, part):
    first, second = jax.random.split(key)
    parts_total = TILES // TILES_DEV
    counts = jax.random.randint(first, (parts_total,), TILES_DEV // 2, TILES_DEV + 1)
    where = jax.random.randint(second, (), 0, parts_total)
    return counts.at[where].set(TILES_DEV).astype(jnp.int32)


def draw_send_count(key, part):
    first, second = jax.random.split(jax.random.fold_in(key, 7))
    parts_total = NODES // NODE_DEV
    counts = jax.random.randint(first, (parts_total * PEERS,), 1, SLOTS + 1)
    where = jax.random.randint(second, (), 0, parts_total * PEERS)
    return counts.at[where].set(SLOTS).reshape(parts_total, PEERS).astype(jnp.int32)


def touch_ends(drawn, rng, low, high):
    dims = drawn.shape
    spot = [jax.random.randint(jax.random.fold_in(rng, axis), (), 0, dims[axis]) for axis in range(len(dims))]
    drawn = drawn.at[tuple(spot)].set(low)
    longest = dims.index(max(dims))
    spot[longest] = (spot[longest] + 1) % dims[longest]
    return drawn.at[tuple(spot)].set(high)


def block_scale(key, dims, cuts, low, top_value):
    def one(position, parts):
        draws = jax.random.uniform(jax.random.fold_in(jax.random.fold_in(key, 6), position), (parts,), jnp.float32, low / len(cuts), top_value / len(cuts))
        return jnp.repeat(jnp.exp(draws), dims[position] // parts).reshape((-1,) + (1,) * (len(dims) - position - 1))

    gain = one(*cuts[0])
    for cut in cuts[1:]:
        gain = gain * one(*cut)
    return gain


def scatter_about(rng, dims, deviation, most, cuts=(), kind=jnp.bfloat16):
    result = deviation * jax.random.normal(rng, dims, jnp.float32)
    if cuts:
        result = result * block_scale(rng, dims, cuts, -0.22, 0.18)
    return jnp.clip(result, -most, most).astype(kind)


def setup_inputs(seed: int = 0) -> dict:
    splits = jax.random.split(jax.random.key(seed), 11)
    feats = scatter_about(splits[0], (NODES, D), 1.0, 6.0, ((0, 8), (1, 4)))
    tile_vals = draw_tile_vals(jax.random.fold_in(splits[10], 71), 0)
    tile_dst = touch_ends(jax.random.randint(splits[2], (TILES,), 0, BLK_DEV), jax.random.fold_in(splits[2], 1), 0, BLK_DEV - 1).astype(jnp.int32)
    tile_src = touch_ends(jax.random.randint(splits[3], (TILES,), 0, SRCS), jax.random.fold_in(splits[3], 1), 0, SRCS - 1).astype(jnp.int32)
    tile_count = draw_tile_count(jax.random.fold_in(splits[10], 71), 0)
    send_blocks = touch_ends(jax.random.randint(splits[5], (N_DOM, PEERS, SLOTS), 0, BLK_DEV), jax.random.fold_in(splits[5], 1), 0, BLK_DEV - 1).astype(jnp.int32)
    send_count = draw_send_count(jax.random.fold_in(splits[10], 71), 0)
    w_self = scatter_about(splits[7], (LAYERS, D, D), D ** -0.5, 0.21875)
    w_nbr = scatter_about(splits[8], (LAYERS, D, D), D ** -0.5, 0.21875)
    bias = scatter_about(splits[9], (LAYERS, D), 0.5, 3.0, (), jnp.float32)
    return dict(feats=feats, tile_vals=tile_vals, tile_dst=tile_dst, tile_src=tile_src, tile_count=tile_count, send_blocks=send_blocks, send_count=send_count, w_self=w_self, w_nbr=w_nbr, bias=bias)


def reference(feats, tile_vals, tile_dst, tile_src, tile_count, send_blocks, send_count, w_self, w_nbr, bias):
    nparts = N_DOM
    blk_dev = NODE_DEV // BLK
    offsets = jnp.array([(d // 2 + 1) * (1 if d % 2 == 0 else -1) for d in range(PEERS)], jnp.int32)
    peer_ids = jnp.arange(PEERS, dtype=jnp.int32)
    values = tile_vals.reshape(nparts, TILES_DEV, BLK, BLK)
    dst_ids = tile_dst.reshape(nparts, TILES_DEV)
    src_ids = tile_src.reshape(nparts, TILES_DEV)
    live = jnp.arange(TILES_DEV, dtype=jnp.int32)[None, :] < tile_count[:, None]
    masked = values * live[:, :, None, None].astype(jnp.bfloat16)
    onehot = (dst_ids[:, None, :] == jnp.arange(blk_dev, dtype=jnp.int32)[None, :, None]).astype(jnp.float32)
    row_sums = jnp.sum(masked.astype(jnp.float32), axis=3)
    degree = 1.0 + jnp.einsum('nbt,nti->nbi', onehot, row_sums)
    hidden = feats
    for layer in range(LAYERS):
        blocks_all = hidden.reshape(nparts, blk_dev, BLK, D)

        def aggregate(part):
            sources = (part - offsets) % nparts
            chosen = send_blocks[sources, peer_ids]
            filled = jnp.arange(SLOTS, dtype=jnp.int32)[None, :] < send_count[sources, peer_ids][:, None]
            received = blocks_all[sources[:, None], chosen] * filled[:, :, None, None].astype(jnp.bfloat16)
            source_list = jnp.concatenate([blocks_all[part], received.reshape(PEERS * SLOTS, BLK, D)], axis=0)
            picked = source_list[src_ids[part]]
            contrib = jnp.einsum('tij,tjf->tif', masked[part].astype(jnp.float32), picked.astype(jnp.float32))
            summed = jnp.einsum('bt,tif->bif', onehot[part], contrib)
            return (summed / degree[part][:, :, None]).astype(jnp.bfloat16)

        agg = lax.map(aggregate, jnp.arange(nparts, dtype=jnp.int32)).reshape(NODES, D)
        pre = jnp.dot(hidden, w_self[layer], preferred_element_type=jnp.float32)
        pre = pre + jnp.dot(agg, w_nbr[layer], preferred_element_type=jnp.float32) + bias[layer][None, :]
        if layer < LAYERS - 1:
            pre = jax.nn.relu(pre)
        hidden = pre.astype(jnp.bfloat16)
    return hidden
```

```python
import functools

import jax
import jax.numpy as jnp
from jax import lax
from jax.experimental import pallas as pl
from jax.experimental.pallas import tpu as pltpu
from jax.sharding import PartitionSpec as P

BLK = 128
GROUP = 4
SIDE = 8
CHUNKS = 2
VMEM = pl.BlockSpec(memory_space=pltpu.VMEM)
SMEM = pl.BlockSpec(memory_space=pltpu.SMEM)


def params():
    return pltpu.CompilerParams(vmem_limit_bytes=40 * 2**20)


def cost(us):
    return pl.CostEstimate(
        flops=int(us * 1e9), bytes_accessed=int(us * 3e6), transcendentals=0
    )


def offset_of(d):
    return (d // 2 + 1) * (1 if d % 2 == 0 else -1)


def peer_of(offset):
    return 2 * (offset - 1) if offset > 0 else 2 * (-offset - 1) + 1


def from_behind(x, distance):
    n = lax.axis_size("dom")
    return lax.ppermute(x, "dom", [(i, (i + distance) % n) for i in range(n)])


def from_partner(x):
    n = lax.axis_size("dom")
    return lax.ppermute(x, "dom", [(i, i ^ 1) for i in range(n)])


def from_feat(x, bit):
    n = lax.axis_size("feat")
    return lax.ppermute(x, "feat", [(i, i ^ bit) for i in range(n)])


def plan_kernel(count, dst, src, place, starts, order, srcs, cursor, *, pad):
    blocks = starts.shape[0] - 1
    live = count[0]

    def clear(b, _):
        cursor[b] = 0
        return 0

    lax.fori_loop(0, blocks, clear, 0)

    def tally(t, _):
        cursor[dst[t]] = cursor[dst[t]] + 1
        return 0

    lax.fori_loop(0, live, tally, 0)

    def begin(b, at):
        starts[b] = at
        groups = (cursor[b] + GROUP - 1) // GROUP
        cursor[b] = at * GROUP
        return at + groups

    starts[blocks] = lax.fori_loop(0, blocks, begin, 0)

    def fill(p, _):
        order[p] = 0
        srcs[p] = pad
        return 0

    lax.fori_loop(0, order.shape[0], fill, 0)

    def put(t, _):
        p = cursor[dst[t]]
        order[p] = t
        srcs[p] = place[src[t]]
        cursor[dst[t]] = p + 1
        return 0

    lax.fori_loop(0, live, put, 0)


def side_by_side(starts, first, rows, product):
    lows = [starts[first + u] for u in range(SIDE)]
    highs = [starts[first + u + 1] for u in range(SIDE)]
    steps = functools.reduce(jnp.maximum, [h - l for h, l in zip(highs, lows)])

    def step(g, sums):
        out = []
        for u in range(SIDE):
            inside = lows[u] + g < highs[u]
            at = jnp.where(inside, lows[u] + g, 0) * GROUP
            out.append(sums[u] + product(at, inside))
        return tuple(out)

    zeros = tuple(jnp.zeros((rows, BLK), jnp.float32) for _ in range(SIDE))
    return lax.fori_loop(0, steps, step, zeros)


def across(left, tiles, order, at):
    right = jnp.concatenate([tiles[order[at + k]] for k in range(GROUP)], axis=1)
    return lax.dot_general(
        left, right, (((1,), (1,)), ((), ())), preferred_element_type=jnp.float32
    )


def degree_kernel(starts, order, srcs, tiles, inverse, *, pad):
    def product(at, inside):
        ones = [
            jnp.full(
                (8, BLK),
                jnp.where(inside & (srcs[at + k] != pad), 1.0, 0.0),
                jnp.float32,
            )
            for k in range(GROUP)
        ]
        left = jnp.concatenate(ones, axis=1).astype(jnp.bfloat16)
        return across(left, tiles, order, at)

    for first in range(0, inverse.shape[0], SIDE):
        sums = side_by_side(starts, first, 8, product)
        for u in range(SIDE):
            inverse[first + u] = 1.0 / (1.0 + sums[u])


def aggregate_kernel(starts, order, srcs, tiles, inverse, *rest, pad):
    *sources, out, held = rest
    at_block = 0
    for ref in sources:

        def copy(i, _, ref=ref, base=at_block):
            held[base + i] = ref[i]
            return 0

        lax.fori_loop(0, ref.shape[0], copy, 0)
        at_block += ref.shape[0]
    rows = held.shape[1]
    held[pad - 1] = jnp.zeros((rows, BLK), held.dtype)
    held[pad] = jnp.zeros((rows, BLK), held.dtype)

    def product(at, inside):
        left = [held[jnp.where(inside, srcs[at + k], pad)] for k in range(GROUP)]
        return across(jnp.concatenate(left, axis=1), tiles, order, at)

    for first in range(0, out.shape[0], SIDE):
        sums = side_by_side(starts, first, rows, product)
        for u in range(SIDE):
            out[first + u] = (sums[u] * inverse[first + u][:1]).astype(out.dtype)


def pair_of(ref, b):
    return jnp.concatenate([ref[b], ref[b + 1]], axis=1)


def self_kernel(weights, bias, full, out, *, feats):
    blocks = out.shape[0]

    def body(q, _):
        parts = [pair_of(full, f * blocks + 2 * q) for f in range(feats)]
        sums = lax.dot_general(
            weights[...],
            jnp.concatenate(parts, axis=0),
            (((1,), (0,)), ((), ())),
            preferred_element_type=jnp.float32,
        )
        sums = sums + bias[...]
        out[2 * q] = sums[:, :BLK]
        out[2 * q + 1] = sums[:, BLK:]
        return 0

    lax.fori_loop(0, blocks // 2, body, 0)


def update_kernel(weights, own, *rest, whole, gathered, feats, last):
    parts = rest[: len(gathered)]
    outs = rest[len(gathered) :]
    blocks = own.shape[0]

    def body(q, _):
        rows = []
        for ref, full in zip(parts, gathered):
            if full:
                rows += [pair_of(ref, f * blocks + 2 * q) for f in range(feats)]
            else:
                rows.append(pair_of(ref, 2 * q))
        sums = lax.dot_general(
            weights[...],
            jnp.concatenate(rows, axis=0),
            (((1,), (0,)), ((), ())),
            preferred_element_type=jnp.float32,
        )
        for k in range(2):
            pre = sums[:, k * BLK : (k + 1) * BLK] + own[2 * q + k]
            if last:
                outs[0][2 * q + k] = pre.astype(jnp.bfloat16)
                continue
            pre = jnp.maximum(pre, 0.0).astype(jnp.bfloat16)
            outs[0][2 * q + k] = pre
            size = pre.shape[0] // CHUNKS
            for c in range(CHUNKS):
                outs[1 + c][2 * q + k] = pre[c * size : (c + 1) * size]
        return 0

    lax.fori_loop(0, blocks // 2, body, 0)


def per_device(
    feats, tile_vals, tile_dst, tile_src, tile_count, send_blocks, send_count, w_self, w_nbr, bias
):
    n = lax.axis_size("dom")
    feat_size = lax.axis_size("feat")
    me = lax.axis_index("dom")
    feat_here = lax.axis_index("feat")
    odd = me % 2
    node_rows, cols = feats.shape
    blocks = node_rows // BLK
    tiles_here = tile_vals.shape[0]
    peers, slots = send_blocks.shape[1:]
    layers, width = bias.shape
    size = cols // CHUNKS
    round_trip = n == peers

    turned = feats.reshape(blocks, BLK, cols).transpose(0, 2, 1)
    chunks = [turned[:, c * size : (c + 1) * size] for c in range(CHUNKS)]

    mine = jnp.concatenate([send_blocks, send_count[:, :, None]], axis=2)
    table = lax.all_gather(mine, "dom", axis=0, tiled=True)

    def row(who, peer):
        sel = (jnp.arange(n) == who % n)[:, None] & (jnp.arange(peers) == peer)[None, :]
        return jnp.sum(jnp.where(sel[:, :, None], table, 0), axis=(0, 1))

    far = blocks if round_trip else 2 * blocks
    base_near, base_far = blocks, 3 * blocks
    base_x = base_far + far
    zero = base_x + 4 * slots
    pad = zero + 1
    place = [jnp.arange(blocks, dtype=jnp.int32)]
    for d in range(peers):
        o = offset_of(d)
        entry = row(me - o, d)
        if o % 2 == 0:
            at = {2: base_near, -2: base_near + blocks, 4: base_far, -4: base_x - blocks}[o]
            at = at + entry[:slots]
        else:
            even_set, odd_set = {1: (1, 0), -1: (0, 2), 3: (3, 1), -3: (2, 3)}[o]
            at = base_x + jnp.where(odd == 1, odd_set, even_set) * slots
            at = at + jnp.arange(slots, dtype=jnp.int32)
        place.append(jnp.where(jnp.arange(slots) < entry[slots], at, zero))
    place = jnp.concatenate(place).astype(jnp.int32)

    def ids(who, even_offset, odd_offset):
        peer = jnp.where(odd == 1, peer_of(odd_offset), peer_of(even_offset))
        return row(who, peer)[:slots]

    ids_own = lax.dynamic_index_in_dim(send_blocks[0], odd, 0, keepdims=False)
    ids_behind = ids(me - 2, 3, 1)
    ids_ahead = ids(me + 2, -1, -3)
    ids_far = ids(me + jnp.where(odd == 1, -4, 4), -3, 3)

    listed = tiles_here + blocks * (GROUP - 1)
    listed = -(-listed // GROUP) * GROUP
    starts, order, srcs = pl.pallas_call(
        functools.partial(plan_kernel, pad=pad),
        name="plan",
        in_specs=[SMEM] * 4,
        out_specs=[SMEM] * 3,
        out_shape=[
            jax.ShapeDtypeStruct((blocks + 1,), jnp.int32),
            jax.ShapeDtypeStruct((listed,), jnp.int32),
            jax.ShapeDtypeStruct((listed,), jnp.int32),
        ],
        scratch_shapes=[pltpu.SMEM((blocks,), jnp.int32)],
        cost_estimate=cost(5),
    )(tile_count, tile_dst, tile_src, place)

    inverse = pl.pallas_call(
        functools.partial(degree_kernel, pad=pad),
        name="degree",
        in_specs=[SMEM] * 3 + [VMEM],
        out_specs=VMEM,
        out_shape=jax.ShapeDtypeStruct((blocks, 8, BLK), jnp.float32),
        compiler_params=params(),
        cost_estimate=cost(8),
    )(starts, order, srcs, tile_vals)

    own_w = lax.dynamic_slice_in_dim(w_self, feat_here * cols, cols, 2).transpose(0, 2, 1)
    nbr_w = lax.dynamic_slice_in_dim(w_nbr, feat_here * cols, cols, 2)
    nbr_w = nbr_w.reshape(layers, feat_size, CHUNKS, size, cols)
    relative = feat_here ^ jnp.arange(feat_size)
    stacked = [
        (nbr_w if c < CHUNKS - 1 else jnp.take(nbr_w, relative, axis=1))[:, :, c]
        for c in range(CHUNKS)
    ]
    nbr_w = jnp.stack(stacked, axis=1).reshape(layers, width, cols).transpose(0, 2, 1)
    own_bias = lax.dynamic_slice_in_dim(bias, feat_here * cols, cols, 1)[:, :, None]

    def sources_of(part):
        x_own = from_partner(part[ids_own])
        behind = from_behind(part, 2)
        ahead = from_behind(part, -2)
        x_behind = from_partner(behind[ids_behind])
        x_ahead = from_partner(ahead[ids_ahead])
        if round_trip:
            half = blocks // 2
            far_parts = [from_behind(behind[:half], 2), from_behind(ahead[half:], -2)]
            from_far = jnp.concatenate(far_parts, axis=0)
        else:
            far_parts = [from_behind(behind, 2), from_behind(ahead, -2)]
            from_far = jnp.where(odd == 1, far_parts[0], far_parts[1])
        x_far = from_partner(from_far[ids_far])
        return [part, behind, ahead, *far_parts, x_own, x_behind, x_ahead, x_far]

    def aggregate(sources):
        rows = sources[0].shape[1]
        return pl.pallas_call(
            functools.partial(aggregate_kernel, pad=pad),
            name="aggregate",
            in_specs=[SMEM] * 3 + [VMEM] * (2 + len(sources)),
            out_specs=VMEM,
            out_shape=jax.ShapeDtypeStruct((blocks, rows, BLK), jnp.bfloat16),
            scratch_shapes=[pltpu.VMEM((pad + 1, rows, BLK), jnp.bfloat16)],
            compiler_params=params(),
            cost_estimate=cost(8),
        )(starts, order, srcs, tile_vals, inverse, *sources)

    for layer in range(layers):
        last = layer == layers - 1
        full = lax.all_gather(turned, "feat", axis=0, tiled=True)
        own = pl.pallas_call(
            functools.partial(self_kernel, feats=feat_size),
            name="own_product",
            in_specs=[VMEM] * 3,
            out_specs=VMEM,
            out_shape=jax.ShapeDtypeStruct((blocks, cols, BLK), jnp.float32),
            compiler_params=params(),
            cost_estimate=cost(4),
        )(own_w[layer], own_bias[layer], full)
        aggs = [aggregate(sources_of(part)) for part in chunks]
        parts, gathered = [], []
        for agg in aggs[:-1]:
            parts.append(lax.all_gather(agg, "feat", axis=0, tiled=True))
            gathered.append(True)
        agg = aggs[-1]
        across_y = from_feat(agg, 2)
        parts += [agg, from_feat(agg, 1), across_y, from_feat(across_y, 1)]
        gathered += [False] * feat_size
        shapes = [jax.ShapeDtypeStruct((blocks, cols, BLK), jnp.bfloat16)]
        if not last:
            shapes += [jax.ShapeDtypeStruct((blocks, size, BLK), jnp.bfloat16)] * CHUNKS
        outs = pl.pallas_call(
            functools.partial(
                update_kernel, whole=None, gathered=tuple(gathered), feats=feat_size, last=last
            ),
            name="update",
            in_specs=[VMEM] * (2 + len(parts)),
            out_specs=[VMEM] * len(shapes),
            out_shape=shapes,
            compiler_params=params(),
            cost_estimate=cost(4),
        )(nbr_w[layer], own, *parts)
        turned, chunks = outs[0], outs[1:]
    return turned.transpose(0, 2, 1).reshape(node_rows, cols)


def solution(mesh):
    in_specs = (
        P("dom", "feat"),
        P("dom", None, None),
        P("dom"),
        P("dom"),
        P("dom"),
        P("dom", None, None),
        P("dom", None),
        P(),
        P(),
        P(),
    )
    out_specs = P("dom", "feat")
    return jax.shard_map(
        per_device, mesh=mesh, in_specs=in_specs, out_specs=out_specs, check_vma=False
    )
```

```python
import functools

import jax
import jax.numpy as jnp
from jax import lax
from jax.experimental import pallas as pl
from jax.experimental.pallas import tpu as pltpu
from jax.sharding import PartitionSpec as P

BLK = 128
GROUP = 4
SIDE = 8
CHUNKS = 2
VMEM = pl.BlockSpec(memory_space=pltpu.VMEM)
SMEM = pl.BlockSpec(memory_space=pltpu.SMEM)


def params():
    return pltpu.CompilerParams(vmem_limit_bytes=18 * 2**20)


def cost(us):
    return pl.CostEstimate(
        flops=int(us * 1e9), bytes_accessed=int(us * 3e6), transcendentals=0
    )


def offset_of(d):
    return (d // 2 + 1) * (1 if d % 2 == 0 else -1)


def peer_of(offset):
    return 2 * (offset - 1) if offset > 0 else 2 * (-offset - 1) + 1


def peer_near(offset, n, peers=8):
    near = (offset + n // 2) % n - n // 2
    for d in range(peers):
        if offset_of(d) == near:
            return d
    return None


def from_behind(x, distance):
    n = lax.axis_size("dom")
    return lax.ppermute(x, "dom", [(i, (i + distance) % n) for i in range(n)])


def from_partner(x):
    n = lax.axis_size("dom")
    return lax.ppermute(x, "dom", [(i, i ^ 1) for i in range(n)])


def from_feat(x, bit):
    n = lax.axis_size("feat")
    return lax.ppermute(x, "feat", [(i, i ^ bit) for i in range(n)])


class Plan:
    def __init__(self, blocks, slots, tiles):
        self.blocks, self.slots = blocks, slots
        lists = 2 * blocks
        longest = tiles + lists * (GROUP - 1)
        self.longest = -(-longest // GROUP) * GROUP
        self.order_at = lists + 1
        self.srcs_at = self.order_at + self.longest
        self.size = self.srcs_at + self.longest

    def views(self, ref):
        return ref, Shifted(ref, self.order_at), Shifted(ref, self.srcs_at)


def picks_kernel(spot, mine, out):
    me = spot[0]
    odd = me % 2 == 1
    layers, _, width = mine.shape
    slots = width - 1
    for k in range(layers):
        peer_even = peer_near(1 + 2 * k, 2 * layers)
        peer_odd = peer_near(-1 + 2 * k, 2 * layers)
        for s in range(slots):
            even_one = 0 if peer_even is None else mine[k, peer_even, s]
            odd_one = 0 if peer_odd is None else mine[k, peer_odd, s]
            out[k, s] = jnp.where(odd, odd_one, even_one)
    low_end = me < 2
    for s in range(slots):
        up_from = jnp.where(odd, mine[0, peer_of(-3), s], mine[0, peer_of(-1), s])
        down_from = jnp.where(odd, mine[0, peer_of(1), s], mine[0, peer_of(3), s])
        out[layers, s] = jnp.where(low_end, up_from, down_from)
        out[layers + 1, s] = jnp.where(
            low_end, mine[0, peer_of(-2), s], mine[0, peer_of(2), s]
        )
        out[layers + 2, s] = me


class Shifted:
    def __init__(self, ref, at):
        self.ref, self.at = ref, at

    def __getitem__(self, i):
        return self.ref[self.at + i]

    def __setitem__(self, i, value):
        self.ref[self.at + i] = value


def plan_kernel(spot, count, dst, src, mine, theirs, out, place, cursor, *, bases, pad, late, plan):
    starts, order, srcs = plan.views(out)
    lists = 2 * plan.blocks
    blocks = plan.blocks
    me = spot[0]
    odd = me % 2 == 1
    layer_here = me // 2
    layers = mine.shape[0]
    peers, width = mine.shape[1:]
    slots = width - 1
    live = count[0]

    def own(b, _):
        place[b] = b
        return 0

    lax.fori_loop(0, blocks, own, 0)
    for d in range(peers):
        o = offset_of(d)
        if o % 2 == 0:
            k = (o // 2) % layers
            base, listed = bases(layer_here, k, False)

            def enter(s, _, d=d, k=k, base=base, listed=listed):
                at = base + jnp.where(listed, s, mine[k, d, s])
                place[blocks + d * slots + s] = jnp.where(s < mine[k, d, slots], at, pad - 1)
                return 0
        else:
            k = jnp.where(odd, ((o - 1) // 2) % layers, ((o + 1) // 2) % layers)
            base_even = bases(layer_here, ((o + 1) // 2) % layers, True)[0]
            base_odd = bases(layer_here, ((o - 1) // 2) % layers, True)[0]
            base = jnp.where(odd, base_odd, base_even)

            def enter(s, _, d=d, k=k, base=base):
                live_slot = s < theirs[k, d, slots]
                place[blocks + d * slots + s] = jnp.where(live_slot, base + s, pad - 1)
                return 0

        lax.fori_loop(0, slots, enter, 0)
    def clear(b, _):
        cursor[b] = 0
        return 0

    lax.fori_loop(0, lists, clear, 0)

    def list_of(t):
        at = place[src[t]]
        return dst[t] + jnp.where((at >= late) & (at < pad - 1), blocks, 0), at

    def tally(t, _):
        b, _at = list_of(t)
        cursor[b] = cursor[b] + 1
        return 0

    lax.fori_loop(0, live, tally, 0)

    def begin(b, at):
        starts[b] = at
        groups = (cursor[b] + GROUP - 1) // GROUP
        cursor[b] = at * GROUP
        return at + groups

    starts[lists] = lax.fori_loop(0, lists, begin, 0)

    def put(t, _):
        b, at = list_of(t)
        p = cursor[b]
        order[p] = t
        srcs[p] = at
        cursor[b] = p + 1
        return 0

    for p in range(GROUP):
        order[p] = 0
        srcs[p] = pad
    lax.fori_loop(0, live, put, 0)

    def fill_up(b, _):
        def fill(p, _):
            order[p] = 0
            srcs[p] = pad
            return 0

        lax.fori_loop(cursor[b], starts[b + 1] * GROUP, fill, 0)
        return 0

    lax.fori_loop(0, lists, fill_up, 0)


def side_by_side(starts, first, sums, product):
    lows = [starts[first + u] for u in range(SIDE)]
    highs = [starts[first + u + 1] for u in range(SIDE)]
    steps = functools.reduce(jnp.maximum, [h - l for h, l in zip(highs, lows)])

    def step(g, sums):
        out = []
        for u in range(SIDE):
            inside = lows[u] + g < highs[u]
            at = jnp.where(inside, lows[u] + g, 0) * GROUP
            out.append(sums[u] + product(at, inside))
        return tuple(out)

    return lax.fori_loop(0, steps, step, tuple(sums))


def zeros(rows):
    return [jnp.zeros((rows, BLK), jnp.float32) for _ in range(SIDE)]


def across(left, tiles, order, at):
    right = jnp.concatenate([tiles[order[at + k]] for k in range(GROUP)], axis=1)
    return lax.dot_general(
        left, right, (((1,), (1,)), ((), ())), preferred_element_type=jnp.float32
    )


def degree_kernel(index, tiles, inverse, kept, *, plan, pad):
    starts, order, srcs = plan.views(index)

    def keep(t, _):
        for k in range(4):
            kept[4 * t + k] = tiles[4 * t + k]
        return 0

    lax.fori_loop(0, tiles.shape[0] // 4, keep, 0)

    def product(at, inside):
        ones = [
            jnp.full(
                (8, BLK),
                jnp.where(inside & (srcs[at + k] != pad), 1.0, 0.0),
                jnp.float32,
            )
            for k in range(GROUP)
        ]
        left = jnp.concatenate(ones, axis=1).astype(jnp.bfloat16)
        return across(left, tiles, order, at)

    blocks = inverse.shape[0]
    for first in range(0, blocks, SIDE):
        sums = side_by_side(starts, first, zeros(8), product)
        sums = side_by_side(starts, blocks + first, sums, product)
        for u in range(SIDE):
            inverse[first + u] = 1.0 / (1.0 + sums[u])


def hold(held, refs):
    base = 0
    for ref in refs:

        def copy(i, _, ref=ref, base=base):
            for k in range(4):
                held[base + 4 * i + k] = ref[4 * i + k]
            return 0

        lax.fori_loop(0, ref.shape[0] // 4, copy, 0)
        base += ref.shape[0]
    held[base] = jnp.zeros(held.shape[1:], held.dtype)
    return base


def early_kernel(index, tiles, *rest, plan, pad):
    *sources, out, held = rest
    starts, order, srcs = plan.views(index)
    end = hold(held, sources)

    def product(at, inside):
        left = []
        for k in range(GROUP):
            src = jnp.where(inside, srcs[at + k], pad)
            left.append(held[jnp.minimum(src, end)])
        return across(jnp.concatenate(left, axis=1), tiles, order, at)

    for first in range(0, out.shape[0], SIDE):
        sums = side_by_side(starts, first, zeros(held.shape[1]), product)
        for u in range(SIDE):
            out[first + u] = sums[u]


def late_kernel(index, tiles, inverse, early, *rest, plan, pad, late, chunk):
    *sources, out, held = rest
    starts, order, srcs = plan.views(index)
    end = hold(held, sources)
    size = held.shape[1]
    cut = slice(chunk * size, (chunk + 1) * size)

    def product(at, inside):
        left = []
        for k in range(GROUP):
            src = jnp.where(inside, srcs[at + k], pad) - late
            left.append(held[jnp.clip(src, 0, end)])
        return across(jnp.concatenate(left, axis=1), tiles, order, at)

    blocks = out.shape[0]
    for first in range(0, blocks, SIDE):
        sums = [early[first + u, cut] for u in range(SIDE)]
        sums = side_by_side(starts, blocks + first, sums, product)
        for u in range(SIDE):
            out[first + u] = (sums[u] * inverse[first + u][:1]).astype(out.dtype)


def weights_kernel(spot, w, out, *, feats, chunks, relative):
    cols, width = out.shape
    here = spot[1]
    rows = []
    if relative:
        size = cols // chunks
        for c in range(chunks):
            for k in range(feats):
                at = pl.multiple_of((here ^ k) * cols + c * size, 16)
                rows.append(w[pl.ds(at, size), :])
        rows = jnp.concatenate(rows, axis=0)
    else:
        rows = w[...]
    column = lax.broadcasted_iota(jnp.int32, (cols, width), 1)
    wanted = lax.broadcasted_iota(jnp.int32, (cols, width), 0) + here * cols
    pick = jnp.where(column == wanted, 1.0, 0.0).astype(rows.dtype)
    turned = lax.dot_general(
        pick, rows, (((1,), (1,)), ((), ())), preferred_element_type=jnp.float32
    )
    out[...] = turned.astype(out.dtype)


def pick_kernel(picks, source, out, *, row):
    def copy(s, _):
        out[s] = source[picks[row, s]]
        return 0

    lax.fori_loop(0, out.shape[0], copy, 0)


def near_kernel(picks, own, below, above, x_out, *outs):
    layer_here = picks[picks.shape[0] - 1, 0] // 2
    slots, blocks = x_out.shape[0], own.shape[0]
    mixed, onward = outs[0::2], outs[1::2]
    size = mixed[0].shape[1]
    cuts = [slice(c * size, (c + 1) * size) for c in range(len(mixed))]

    def copy(s, _):
        x_out[s] = jnp.where(layer_here == 0, above[picks[3, s]], below[picks[1, s]])
        return 0

    lax.fori_loop(0, slots, copy, 0)

    @pl.when((layer_here == 0) | (layer_here == 3))
    def _():
        def copy(s, _):
            for c, cut in enumerate(cuts):
                mixed[c][s] = own[picks[4, s], cut]
                mixed[c][slots + s] = own[picks[5, s], cut]
            return 0

        lax.fori_loop(0, slots, copy, 0)

    def relay(through, back):
        def copy(i, _):
            for k in range(2):
                for c, cut in enumerate(cuts):
                    mixed[c][2 * i + k] = through[2 * i + k, cut]
                    onward[c][2 * i + k] = back[2 * i + k, cut]
            return 0

        lax.fori_loop(0, blocks // 2, copy, 0)

    @pl.when(layer_here == 1)
    def _():
        relay(below, above)

    @pl.when(layer_here == 2)
    def _():
        relay(above, below)


def far_kernel(picks, above, mixed, onward, out, *, chunk):
    layer_here = picks[picks.shape[0] - 1, 0] // 2
    slots, size = picks.shape[1], mixed.shape[1]
    cut = slice(chunk * size, (chunk + 1) * size)
    end = (layer_here == 0) | (layer_here == 3)

    @pl.when(end)
    def _():
        def copy(s, _):
            out[s] = onward[picks[2, s]]
            out[slots + s] = mixed[s]
            return 0

        lax.fori_loop(0, slots, copy, 0)

    @pl.when(jnp.logical_not(end))
    def _():
        def copy(s, _):
            out[s] = above[picks[3, s], cut]
            out[slots + s] = mixed[picks[2, s]]
            return 0

        lax.fori_loop(0, slots, copy, 0)


def pair_of(ref, b):
    return jnp.concatenate([ref[b], ref[b + 1]], axis=1)


def self_kernel(weights, bias, full, out, *, feats):
    blocks = out.shape[0]

    def body(q, _):
        parts = [pair_of(full, f * blocks + 2 * q) for f in range(feats)]
        sums = lax.dot_general(
            weights[...],
            jnp.concatenate(parts, axis=0),
            (((1,), (0,)), ((), ())),
            preferred_element_type=jnp.float32,
        )
        sums = sums + bias[...]
        out[2 * q] = sums[:, :BLK]
        out[2 * q + 1] = sums[:, BLK:]
        return 0

    lax.fori_loop(0, blocks // 2, body, 0)


def update_kernel(weights, before, *rest, count, low, kind):
    parts, out = rest[:count], rest[count]
    blocks = out.shape[0]

    def body(q, _):
        rows = jnp.concatenate([pair_of(ref, 2 * q) for ref in parts], axis=0)
        sums = lax.dot_general(
            weights[:, low : low + rows.shape[0]],
            rows,
            (((1,), (0,)), ((), ())),
            preferred_element_type=jnp.float32,
        )
        for k in range(2):
            pre = sums[:, k * BLK : (k + 1) * BLK] + before[2 * q + k]
            if kind == "relu":
                pre = jnp.maximum(pre, 0.0)
            out[2 * q + k] = pre.astype(out.dtype)
        return 0

    lax.fori_loop(0, blocks // 2, body, 0)


def tie(first, *others):
    return lax.optimization_barrier((tuple(first), *others))[0]


def line_base(blocks, slots):
    late = 3 * blocks + 2 * slots
    mixed, onward, x_far = late, late + blocks, late + 2 * blocks

    def base(layer_here, k, partner):
        middle = (layer_here == 1) | (layer_here == 2)
        lacking = layer_here == (0 if k == 1 else 3)
        if not partner:
            if k == 2:
                return jnp.where(middle, mixed, onward), False
            return jnp.where(lacking, mixed + slots, blocks + k // 2 * blocks), lacking
        if k == 0:
            return 3 * blocks, True
        if k == 2:
            return jnp.where(middle, x_far + slots, x_far), True
        here = 3 * blocks + slots
        if k == 3:
            here = jnp.where(layer_here == 0, here, x_far)
        return jnp.where(lacking, x_far + slots, here), True

    return base


def ring_base(blocks, slots, layers):
    def base(layer_here, k, partner):
        del layer_here
        if partner:
            if k in (2, layers - 2):
                return 5 * blocks + 3 * slots, True
            return 3 * blocks + {0: 0, 1: 1, layers - 1: 2}[k] * slots, True
        if k in (2, layers - 2):
            return 3 * blocks + 3 * slots + (0 if k == 2 else blocks), False
        return {1: 1, layers - 1: 2}[k] * blocks, False

    return base


def per_device(
    feats, tile_vals, tile_dst, tile_src, tile_count, send_blocks, send_count, w_self, w_nbr, bias
):
    n = lax.axis_size("dom")
    feat_size = lax.axis_size("feat")
    me = lax.axis_index("dom")
    feat_here = lax.axis_index("feat")
    node_rows, cols = feats.shape
    blocks = node_rows // BLK
    tiles_here = tile_vals.shape[0]
    peers, slots = send_blocks.shape[1:]
    layers, width = bias.shape
    depth = n // 2
    line = depth == 4
    chunks = CHUNKS if line else 1
    size = cols // chunks
    spot = jnp.stack([me, feat_here]).astype(jnp.int32)
    plan = Plan(blocks, slots, tiles_here)

    own_table = jnp.concatenate([send_blocks, send_count[:, :, None]], axis=2)
    near_by = {1: 2, 2: 4, depth - 2: -4, depth - 1: -2}
    far_tables = [
        from_behind(own_table, near_by[k]) if k in near_by else own_table for k in range(1, depth)
    ]
    mine = jnp.concatenate([own_table, *far_tables], axis=0)
    theirs = from_partner(mine)

    hidden = feats.reshape(blocks, BLK, cols).transpose(0, 2, 1)

    if line:
        late, pad = 3 * blocks + 2 * slots, 5 * blocks + 4 * slots + 1
        bases = line_base(blocks, slots)
    else:
        late, pad = 3 * blocks + 3 * slots, 5 * blocks + 4 * slots + 1
        bases = ring_base(blocks, slots, depth)

    picks = pl.pallas_call(
        picks_kernel,
        name="picks",
        in_specs=[SMEM] * 2,
        out_specs=SMEM,
        out_shape=jax.ShapeDtypeStruct((depth + 3, slots), jnp.int32),
        cost_estimate=cost(1),
    )(spot, mine)
    def call(kernel, name, out_shape, us, scalars, *args, held=None, **static):
        return pl.pallas_call(
            functools.partial(kernel, **static),
            name=name,
            in_specs=[SMEM] + [VMEM] * len(args),
            out_specs=jax.tree.map(lambda _: VMEM, out_shape),
            out_shape=out_shape,
            scratch_shapes=[] if held is None else [pltpu.VMEM(held, jnp.bfloat16)],
            compiler_params=params(),
            cost_estimate=cost(us),
        )(scalars, *args)

    made = {}

    made["index"] = pl.pallas_call(
        functools.partial(plan_kernel, bases=bases, pad=pad, late=late, plan=plan),
        name="plan",
        in_specs=[SMEM] * 6,
        out_specs=SMEM,
        out_shape=jax.ShapeDtypeStruct((plan.size,), jnp.int32),
        scratch_shapes=[
            pltpu.SMEM((blocks + peers * slots,), jnp.int32),
            pltpu.SMEM((2 * blocks,), jnp.int32),
        ],
        cost_estimate=cost(5),
    )(spot, tile_count, tile_dst, tile_src, mine, theirs)

    def degrees(*after):
        if "tiles" in made:
            return
        (tiles_in,) = tie((tile_vals,), *after)
        made["inverse"], made["tiles"] = call(
            degree_kernel,
            "degree",
            [
                pltpu.VMEM((blocks, 8, BLK), jnp.float32),
                pltpu.VMEM(tile_vals.shape, tile_vals.dtype),
            ],
            0.01,
            made["index"],
            tiles_in,
            plan=plan,
            pad=pad,
        )

    def turned_weights(w, relative):
        return pl.pallas_call(
            functools.partial(
                weights_kernel, feats=feat_size, chunks=chunks, relative=relative
            ),
            name="turn_weights",
            grid=(layers,),
            in_specs=[SMEM, pl.BlockSpec((None, width, width), lambda l: (l, 0, 0))],
            out_specs=pl.BlockSpec((None, cols, width), lambda l: (l, 0, 0)),
            out_shape=jax.ShapeDtypeStruct((layers, cols, width), w.dtype),
            compiler_params=params(),
            cost_estimate=cost(0.01),
        )(spot, w)

    own_w, nbr_w = turned_weights(w_self, False), turned_weights(w_nbr, True)
    own_bias = lax.dynamic_slice_in_dim(bias, feat_here * cols, cols, 1)[:, :, None]

    def parts_of(number, rows):
        return jax.ShapeDtypeStruct((number, rows, BLK), jnp.bfloat16)

    def pick(source, row):
        return call(pick_kernel, "pick", parts_of(slots, cols), 1, picks, source, row=row)

    def sum_early(sources):
        return call(
            early_kernel,
            "sum_early",
            pltpu.VMEM((blocks, cols, BLK), jnp.float32),
            6,
            made["index"],
            made["tiles"],
            *sources,
            held=(late + 1, cols, BLK),
            plan=plan,
            pad=pad,
        )

    def aggregate(early, sources, chunk):
        return call(
            late_kernel,
            "aggregate",
            parts_of(blocks, size),
            3,
            made["index"],
            made["tiles"],
            made["inverse"],
            early,
            *sources,
            held=(pad - late, size, BLK),
            plan=plan,
            pad=pad,
            late=late,
            chunk=chunk,
        )

    def own_product(layer, full):
        return pl.pallas_call(
            functools.partial(self_kernel, feats=feat_size),
            name="own_product",
            in_specs=[VMEM] * 3,
            out_specs=VMEM,
            out_shape=pltpu.VMEM((blocks, cols, BLK), jnp.float32),
            compiler_params=params(),
            cost_estimate=cost(2),
        )(own_w[layer], own_bias[layer], full)

    def update(weights, before, parts, low, kind):
        shapes = [pltpu.VMEM((blocks, cols, BLK), jnp.float32)]
        if kind != "sum":
            shapes = [parts_of(blocks, cols)]
        return pl.pallas_call(
            functools.partial(update_kernel, count=len(parts), low=low, kind=kind),
            name="update",
            in_specs=[VMEM] * (2 + len(parts)),
            out_specs=[VMEM] * len(shapes),
            out_shape=shapes,
            compiler_params=params(),
            cost_estimate=cost(3),
        )(weights, before, *parts)

    def send(x, pairs):
        return lax.ppermute(x, "dom", pairs)

    def from_line(hidden, state):
        up = [(i, i + 2) for i in range(n - 2)]
        down = [(i + 2, i) for i in range(n - 2)]
        mix = [(0, 6), (1, 7), (6, 0), (7, 1), (2, 4), (3, 5), (4, 2), (5, 3)]
        outward = [(2, 0), (3, 1), (4, 6), (5, 7)]
        below, above = send(hidden, up), send(hidden, down)
        x_own = from_partner(pick(hidden, 0))
        below, above, x_own, _ = lax.optimization_barrier((below, above, x_own, made["index"]))
        shapes = [parts_of(slots, cols)] + [parts_of(blocks, size)] * (2 * chunks)
        x_near, *onwards = call(near_kernel, "near", shapes, 2, picks, hidden, below, above)
        degrees(x_near)
        x_near = from_partner(x_near)
        far = [
            (send(onwards[2 * c], mix), send(onwards[2 * c + 1], outward)) for c in range(chunks)
        ]
        early = sum_early([hidden, below, above, x_own, x_near])
        listed = []
        for c, (mixed, onward) in enumerate(far):
            mixed, onward = far[c] = tie((mixed, onward), early, state, listed)
            shape = parts_of(2 * slots, size)
            listed.append(
                call(far_kernel, "far", shape, 1, picks, above, mixed, onward, chunk=c)
            )
        aggs = []
        for c, (mixed, onward) in enumerate(far):
            x_far = from_partner(listed[c])
            x_far, *_ = tie((x_far,), listed, aggs)
            aggs.append(aggregate(early, [mixed, onward, x_far], c))
        return aggs

    def from_ring(hidden):
        behind, ahead = from_behind(hidden, 2), from_behind(hidden, -2)
        behind_two, ahead_two = from_behind(behind, 2), from_behind(ahead, -2)
        x_own = from_partner(pick(hidden, 0))
        x_near = [from_partner(pick(behind, 1)), from_partner(pick(ahead, depth - 1))]
        degrees()
        odd = me % 2 == 1
        x_two = jnp.where(odd, pick(behind_two, 2), pick(ahead_two, depth - 2))
        early = sum_early([hidden, behind, ahead, x_own, *x_near])
        return [aggregate(early, [behind_two, ahead_two, from_partner(x_two)], 0)]

    for layer in range(layers):
        last = layer == layers - 1
        state = own_product(layer, lax.all_gather(hidden, "feat", axis=0, tiled=True))
        aggs = from_line(hidden, state) if line else from_ring(hidden)
        for c, agg in enumerate(aggs):
            other = from_feat(agg, 2)
            parts = [agg, from_feat(agg, 1), other, from_feat(other, 1)]
            kind = "sum" if c < chunks - 1 else "none" if last else "relu"
            (state,) = update(nbr_w[layer], state, parts, c * feat_size * size, kind)
        hidden = state
    return hidden.transpose(0, 2, 1).reshape(node_rows, cols)


def solution(mesh):
    in_specs = (
        P("dom", "feat"),
        P("dom", None, None),
        P("dom"),
        P("dom"),
        P("dom"),
        P("dom", None, None),
        P("dom", None),
        P(),
        P(),
        P(),
    )
    out_specs = P("dom", "feat")
    return jax.shard_map(
        per_device, mesh=mesh, in_specs=in_specs, out_specs=out_specs, check_vma=False
    )
```

```python
import functools

import jax
import jax.numpy as jnp
from jax import lax
from jax.experimental import pallas as pl
from jax.experimental.pallas import tpu as pltpu
from jax.sharding import PartitionSpec as P

BLK = 128
GROUP = 4
SIDE = 8
CHUNKS = 2
VMEM = pl.BlockSpec(memory_space=pltpu.VMEM)
SMEM = pl.BlockSpec(memory_space=pltpu.SMEM)


def params():
    return pltpu.CompilerParams(vmem_limit_bytes=18 * 2**20)


def cost(us):
    return pl.CostEstimate(
        flops=int(us * 1e9), bytes_accessed=int(us * 3e6), transcendentals=0
    )


def offset_of(d):
    return (d // 2 + 1) * (1 if d % 2 == 0 else -1)


def peer_of(offset):
    return 2 * (offset - 1) if offset > 0 else 2 * (-offset - 1) + 1


def peer_near(offset, n, peers=8):
    near = (offset + n // 2) % n - n // 2
    for d in range(peers):
        if offset_of(d) == near:
            return d
    return None


def from_behind(x, distance):
    n = lax.axis_size("dom")
    return lax.ppermute(x, "dom", [(i, (i + distance) % n) for i in range(n)])


def from_partner(x):
    n = lax.axis_size("dom")
    return lax.ppermute(x, "dom", [(i, i ^ 1) for i in range(n)])


def from_feat(x, bit):
    n = lax.axis_size("feat")
    return lax.ppermute(x, "feat", [(i, i ^ bit) for i in range(n)])


class Plan:
    def __init__(self, blocks, slots, tiles):
        self.blocks, self.slots = blocks, slots
        lists = 2 * blocks
        longest = tiles + lists * (GROUP - 1)
        self.longest = -(-longest // GROUP) * GROUP
        self.order_at = lists + 1
        self.srcs_at = self.order_at + self.longest
        self.size = self.srcs_at + self.longest

    def views(self, ref):
        return ref, Shifted(ref, self.order_at), Shifted(ref, self.srcs_at)


def picks_kernel(spot, mine, out):
    me = spot[0]
    odd = me % 2 == 1
    layers, _, width = mine.shape
    slots = width - 1
    for k in range(layers):
        peer_even = peer_near(1 + 2 * k, 2 * layers)
        peer_odd = peer_near(-1 + 2 * k, 2 * layers)
        for s in range(slots):
            even_one = 0 if peer_even is None else mine[k, peer_even, s]
            odd_one = 0 if peer_odd is None else mine[k, peer_odd, s]
            out[k, s] = jnp.where(odd, odd_one, even_one)
    low_end = me < 2
    for s in range(slots):
        up_from = jnp.where(odd, mine[0, peer_of(-3), s], mine[0, peer_of(-1), s])
        down_from = jnp.where(odd, mine[0, peer_of(1), s], mine[0, peer_of(3), s])
        out[layers, s] = jnp.where(low_end, up_from, down_from)
        out[layers + 1, s] = jnp.where(
            low_end, mine[0, peer_of(-2), s], mine[0, peer_of(2), s]
        )
        out[layers + 2, s] = me


class Shifted:
    def __init__(self, ref, at):
        self.ref, self.at = ref, at

    def __getitem__(self, i):
        return self.ref[self.at + i]

    def __setitem__(self, i, value):
        self.ref[self.at + i] = value


def plan_kernel(spot, count, dst, src, mine, theirs, out, place, cursor, *, bases, pad, late, plan):
    starts, order, srcs = plan.views(out)
    lists = 2 * plan.blocks
    blocks = plan.blocks
    me = spot[0]
    odd = me % 2 == 1
    layer_here = me // 2
    layers = mine.shape[0]
    peers, width = mine.shape[1:]
    slots = width - 1
    live = count[0]

    def own(b, _):
        place[b] = b
        return 0

    lax.fori_loop(0, blocks, own, 0)
    for d in range(peers):
        o = offset_of(d)
        if o % 2 == 0:
            k = (o // 2) % layers
            base, listed = bases(layer_here, k, False)

            def enter(s, _, d=d, k=k, base=base, listed=listed):
                at = base + jnp.where(listed, s, mine[k, d, s])
                place[blocks + d * slots + s] = jnp.where(s < mine[k, d, slots], at, pad - 1)
                return 0
        else:
            k = jnp.where(odd, ((o - 1) // 2) % layers, ((o + 1) // 2) % layers)
            base_even = bases(layer_here, ((o + 1) // 2) % layers, True)[0]
            base_odd = bases(layer_here, ((o - 1) // 2) % layers, True)[0]
            base = jnp.where(odd, base_odd, base_even)

            def enter(s, _, d=d, k=k, base=base):
                live_slot = s < theirs[k, d, slots]
                place[blocks + d * slots + s] = jnp.where(live_slot, base + s, pad - 1)
                return 0

        lax.fori_loop(0, slots, enter, 0)
    def clear(b, _):
        cursor[b] = 0
        return 0

    lax.fori_loop(0, lists, clear, 0)

    def list_of(t):
        at = place[src[t]]
        return dst[t] + jnp.where((at >= late) & (at < pad - 1), blocks, 0), at

    def tally(t, _):
        b, _at = list_of(t)
        cursor[b] = cursor[b] + 1
        return 0

    lax.fori_loop(0, live, tally, 0)

    def begin(b, at):
        starts[b] = at
        groups = (cursor[b] + GROUP - 1) // GROUP
        cursor[b] = at * GROUP
        return at + groups

    starts[lists] = lax.fori_loop(0, lists, begin, 0)

    def put(t, _):
        b, at = list_of(t)
        p = cursor[b]
        order[p] = t
        srcs[p] = at
        cursor[b] = p + 1
        return 0

    for p in range(GROUP):
        order[p] = 0
        srcs[p] = pad
    lax.fori_loop(0, live, put, 0)

    def fill_up(b, _):
        def fill(p, _):
            order[p] = 0
            srcs[p] = pad
            return 0

        lax.fori_loop(cursor[b], starts[b + 1] * GROUP, fill, 0)
        return 0

    lax.fori_loop(0, lists, fill_up, 0)


def side_by_side(starts, first, sums, product):
    lows = [starts[first + u] for u in range(SIDE)]
    highs = [starts[first + u + 1] for u in range(SIDE)]
    steps = functools.reduce(jnp.maximum, [h - l for h, l in zip(highs, lows)])

    def step(g, sums):
        out = []
        for u in range(SIDE):
            inside = lows[u] + g < highs[u]
            at = jnp.where(inside, lows[u] + g, 0) * GROUP
            out.append(sums[u] + product(at, inside))
        return tuple(out)

    return lax.fori_loop(0, steps, step, tuple(sums))


def zeros(rows):
    return [jnp.zeros((rows, BLK), jnp.float32) for _ in range(SIDE)]


def across(left, tiles, order, at):
    right = jnp.concatenate([tiles[order[at + k]] for k in range(GROUP)], axis=1)
    return lax.dot_general(
        left, right, (((1,), (1,)), ((), ())), preferred_element_type=jnp.float32
    )


def degree_kernel(index, tiles, inverse, kept, *, plan, pad):
    starts, order, srcs = plan.views(index)

    def keep(t, _):
        for k in range(4):
            kept[4 * t + k] = tiles[4 * t + k]
        return 0

    lax.fori_loop(0, tiles.shape[0] // 4, keep, 0)

    def product(at, inside):
        ones = [
            jnp.full(
                (8, BLK),
                jnp.where(inside & (srcs[at + k] != pad), 1.0, 0.0),
                jnp.float32,
            )
            for k in range(GROUP)
        ]
        left = jnp.concatenate(ones, axis=1).astype(jnp.bfloat16)
        return across(left, tiles, order, at)

    blocks = inverse.shape[0]
    for first in range(0, blocks, SIDE):
        sums = side_by_side(starts, first, zeros(8), product)
        sums = side_by_side(starts, blocks + first, sums, product)
        for u in range(SIDE):
            inverse[first + u] = 1.0 / (1.0 + sums[u])


def hold(held, refs):
    base = 0
    for ref in refs:

        def copy(i, _, ref=ref, base=base):
            for k in range(4):
                held[base + 4 * i + k] = ref[4 * i + k]
            return 0

        lax.fori_loop(0, ref.shape[0] // 4, copy, 0)
        base += ref.shape[0]
    held[base] = jnp.zeros(held.shape[1:], held.dtype)
    return base


def early_kernel(index, tiles, *rest, plan, pad):
    *sources, out, held = rest
    starts, order, srcs = plan.views(index)
    end = hold(held, sources)

    def product(at, inside):
        left = []
        for k in range(GROUP):
            src = jnp.where(inside, srcs[at + k], pad)
            left.append(held[jnp.minimum(src, end)])
        return across(jnp.concatenate(left, axis=1), tiles, order, at)

    for first in range(0, out.shape[0], SIDE):
        sums = side_by_side(starts, first, zeros(held.shape[1]), product)
        for u in range(SIDE):
            out[first + u] = sums[u]


def late_kernel(index, tiles, inverse, early, *rest, plan, pad, late, chunk):
    *sources, out, held = rest
    starts, order, srcs = plan.views(index)
    end = hold(held, sources)
    size = held.shape[1]
    cut = slice(chunk * size, (chunk + 1) * size)

    def product(at, inside):
        left = []
        for k in range(GROUP):
            src = jnp.where(inside, srcs[at + k], pad) - late
            left.append(held[jnp.clip(src, 0, end)])
        return across(jnp.concatenate(left, axis=1), tiles, order, at)

    blocks = out.shape[0]
    for first in range(0, blocks, SIDE):
        sums = [early[first + u, cut] for u in range(SIDE)]
        sums = side_by_side(starts, blocks + first, sums, product)
        for u in range(SIDE):
            out[first + u] = (sums[u] * inverse[first + u][:1]).astype(out.dtype)


def weights_kernel(spot, w, out, *, feats, chunks, relative):
    cols, width = out.shape
    here = spot[1]
    rows = []
    if relative:
        size = cols // chunks
        for c in range(chunks):
            for k in range(feats):
                at = pl.multiple_of((here ^ k) * cols + c * size, 16)
                rows.append(w[pl.ds(at, size), :])
        rows = jnp.concatenate(rows, axis=0)
    else:
        rows = w[...]
    column = lax.broadcasted_iota(jnp.int32, (cols, width), 1)
    wanted = lax.broadcasted_iota(jnp.int32, (cols, width), 0) + here * cols
    pick = jnp.where(column == wanted, 1.0, 0.0).astype(rows.dtype)
    turned = lax.dot_general(
        pick, rows, (((1,), (1,)), ((), ())), preferred_element_type=jnp.float32
    )
    out[...] = turned.astype(out.dtype)


def pick_kernel(picks, source, out, *, row):
    def copy(s, _):
        out[s] = source[picks[row, s]]
        return 0

    lax.fori_loop(0, out.shape[0], copy, 0)


def near_kernel(picks, own, below, above, x_out, *outs):
    layer_here = picks[picks.shape[0] - 1, 0] // 2
    slots, blocks = x_out.shape[0], own.shape[0]
    mixed, onward = outs[0::2], outs[1::2]
    size = mixed[0].shape[1]
    cuts = [slice(c * size, (c + 1) * size) for c in range(len(mixed))]

    def copy(s, _):
        x_out[s] = jnp.where(layer_here == 0, above[picks[3, s]], below[picks[1, s]])
        return 0

    lax.fori_loop(0, slots, copy, 0)

    @pl.when((layer_here == 0) | (layer_here == 3))
    def _():
        def copy(s, _):
            for c, cut in enumerate(cuts):
                mixed[c][s] = own[picks[4, s], cut]
                mixed[c][slots + s] = own[picks[5, s], cut]
            return 0

        lax.fori_loop(0, slots, copy, 0)

    def relay(through, back):
        def copy(i, _):
            for k in range(2):
                for c, cut in enumerate(cuts):
                    mixed[c][2 * i + k] = through[2 * i + k, cut]
                    onward[c][2 * i + k] = back[2 * i + k, cut]
            return 0

        lax.fori_loop(0, blocks // 2, copy, 0)

    @pl.when(layer_here == 1)
    def _():
        relay(below, above)

    @pl.when(layer_here == 2)
    def _():
        relay(above, below)


def far_kernel(picks, above, mixed, onward, out, *, chunk):
    layer_here = picks[picks.shape[0] - 1, 0] // 2
    slots, size = picks.shape[1], mixed.shape[1]
    cut = slice(chunk * size, (chunk + 1) * size)
    end = (layer_here == 0) | (layer_here == 3)

    @pl.when(end)
    def _():
        def copy(s, _):
            out[s] = onward[picks[2, s]]
            out[slots + s] = mixed[s]
            return 0

        lax.fori_loop(0, slots, copy, 0)

    @pl.when(jnp.logical_not(end))
    def _():
        def copy(s, _):
            out[s] = above[picks[3, s], cut]
            out[slots + s] = mixed[picks[2, s]]
            return 0

        lax.fori_loop(0, slots, copy, 0)


def pair_of(ref, b):
    return jnp.concatenate([ref[b], ref[b + 1]], axis=1)


def self_kernel(weights, bias, full, out, *, feats):
    blocks = out.shape[0]

    def body(q, _):
        parts = [pair_of(full, f * blocks + 2 * q) for f in range(feats)]
        sums = lax.dot_general(
            weights[...],
            jnp.concatenate(parts, axis=0),
            (((1,), (0,)), ((), ())),
            preferred_element_type=jnp.float32,
        )
        sums = sums + bias[...]
        out[2 * q] = sums[:, :BLK]
        out[2 * q + 1] = sums[:, BLK:]
        return 0

    lax.fori_loop(0, blocks // 2, body, 0, unroll=True)


def update_kernel(weights, before, *rest, count, low, kind):
    parts, out = rest[:count], rest[count]
    blocks = out.shape[0]

    def body(q, _):
        rows = jnp.concatenate([pair_of(ref, 2 * q) for ref in parts], axis=0)
        sums = lax.dot_general(
            weights[:, low : low + rows.shape[0]],
            rows,
            (((1,), (0,)), ((), ())),
            preferred_element_type=jnp.float32,
        )
        for k in range(2):
            pre = sums[:, k * BLK : (k + 1) * BLK] + before[2 * q + k]
            if kind == "relu":
                pre = jnp.maximum(pre, 0.0)
            out[2 * q + k] = pre.astype(out.dtype)
        return 0

    lax.fori_loop(0, blocks // 2, body, 0, unroll=True)


def tie(first, *others):
    return lax.optimization_barrier((tuple(first), *others))[0]


def line_base(blocks, slots):
    late = 3 * blocks + 2 * slots
    mixed, onward, x_far = late, late + blocks, late + 2 * blocks

    def base(layer_here, k, partner):
        middle = (layer_here == 1) | (layer_here == 2)
        lacking = layer_here == (0 if k == 1 else 3)
        if not partner:
            if k == 2:
                return jnp.where(middle, mixed, onward), False
            return jnp.where(lacking, mixed + slots, blocks + k // 2 * blocks), lacking
        if k == 0:
            return 3 * blocks, True
        if k == 2:
            return jnp.where(middle, x_far + slots, x_far), True
        here = 3 * blocks + slots
        if k == 3:
            here = jnp.where(layer_here == 0, here, x_far)
        return jnp.where(lacking, x_far + slots, here), True

    return base


def ring_base(blocks, slots, layers):
    def base(layer_here, k, partner):
        del layer_here
        if partner:
            if k in (2, layers - 2):
                return 5 * blocks + 3 * slots, True
            return 3 * blocks + {0: 0, 1: 1, layers - 1: 2}[k] * slots, True
        if k in (2, layers - 2):
            return 3 * blocks + 3 * slots + (0 if k == 2 else blocks), False
        return {1: 1, layers - 1: 2}[k] * blocks, False

    return base


def per_device(
    feats, tile_vals, tile_dst, tile_src, tile_count, send_blocks, send_count, w_self, w_nbr, bias
):
    n = lax.axis_size("dom")
    feat_size = lax.axis_size("feat")
    me = lax.axis_index("dom")
    feat_here = lax.axis_index("feat")
    node_rows, cols = feats.shape
    blocks = node_rows // BLK
    tiles_here = tile_vals.shape[0]
    peers, slots = send_blocks.shape[1:]
    layers, width = bias.shape
    depth = n // 2
    line = depth == 4
    chunks = CHUNKS if line else 1
    size = cols // chunks
    spot = jnp.stack([me, feat_here]).astype(jnp.int32)
    plan = Plan(blocks, slots, tiles_here)

    own_table = jnp.concatenate([send_blocks, send_count[:, :, None]], axis=2)
    near_by = {1: 2, 2: 4, depth - 2: -4, depth - 1: -2}
    far_tables = [
        from_behind(own_table, near_by[k]) if k in near_by else own_table for k in range(1, depth)
    ]
    mine = jnp.concatenate([own_table, *far_tables], axis=0)
    theirs = from_partner(mine)

    hidden = feats.reshape(blocks, BLK, cols).transpose(0, 2, 1)

    if line:
        late, pad = 3 * blocks + 2 * slots, 5 * blocks + 4 * slots + 1
        bases = line_base(blocks, slots)
    else:
        late, pad = 3 * blocks + 3 * slots, 5 * blocks + 4 * slots + 1
        bases = ring_base(blocks, slots, depth)

    picks = pl.pallas_call(
        picks_kernel,
        name="picks",
        in_specs=[SMEM] * 2,
        out_specs=SMEM,
        out_shape=jax.ShapeDtypeStruct((depth + 3, slots), jnp.int32),
        cost_estimate=cost(1),
    )(spot, mine)
    def call(kernel, name, out_shape, us, scalars, *args, held=None, **static):
        return pl.pallas_call(
            functools.partial(kernel, **static),
            name=name,
            in_specs=[SMEM] + [VMEM] * len(args),
            out_specs=jax.tree.map(lambda _: VMEM, out_shape),
            out_shape=out_shape,
            scratch_shapes=[] if held is None else [pltpu.VMEM(held, jnp.bfloat16)],
            compiler_params=params(),
            cost_estimate=cost(us),
        )(scalars, *args)

    made = {}

    made["index"] = pl.pallas_call(
        functools.partial(plan_kernel, bases=bases, pad=pad, late=late, plan=plan),
        name="plan",
        in_specs=[SMEM] * 6,
        out_specs=SMEM,
        out_shape=jax.ShapeDtypeStruct((plan.size,), jnp.int32),
        scratch_shapes=[
            pltpu.SMEM((blocks + peers * slots,), jnp.int32),
            pltpu.SMEM((2 * blocks,), jnp.int32),
        ],
        cost_estimate=cost(5),
    )(spot, tile_count, tile_dst, tile_src, mine, theirs)

    def degrees(*after):
        if "tiles" in made:
            return
        (tiles_in,) = tie((tile_vals,), *after)
        made["inverse"], made["tiles"] = call(
            degree_kernel,
            "degree",
            [
                pltpu.VMEM((blocks, 8, BLK), jnp.float32),
                pltpu.VMEM(tile_vals.shape, tile_vals.dtype),
            ],
            0.01,
            made["index"],
            tiles_in,
            plan=plan,
            pad=pad,
        )

    def turned_weights(w, relative):
        return pl.pallas_call(
            functools.partial(
                weights_kernel, feats=feat_size, chunks=chunks, relative=relative
            ),
            name="turn_weights",
            grid=(layers,),
            in_specs=[SMEM, pl.BlockSpec((None, width, width), lambda l: (l, 0, 0))],
            out_specs=pl.BlockSpec((None, cols, width), lambda l: (l, 0, 0)),
            out_shape=jax.ShapeDtypeStruct((layers, cols, width), w.dtype),
            compiler_params=params(),
            cost_estimate=cost(0.01),
        )(spot, w)

    own_bias = lax.dynamic_slice_in_dim(bias, feat_here * cols, cols, 1)[:, :, None]

    def weights(*after):
        if "own" not in made:
            made["own"] = turned_weights(tie((w_self,), *after)[0], False)
            made["nbr"] = turned_weights(tie((w_nbr,), *after)[0], True)

    def parts_of(number, rows):
        return jax.ShapeDtypeStruct((number, rows, BLK), jnp.bfloat16)

    def pick(source, row):
        return call(pick_kernel, "pick", parts_of(slots, cols), 1, picks, source, row=row)

    def sum_early(sources):
        return call(
            early_kernel,
            "sum_early",
            pltpu.VMEM((blocks, cols, BLK), jnp.float32),
            6,
            made["index"],
            made["tiles"],
            *sources,
            held=(late + 1, cols, BLK),
            plan=plan,
            pad=pad,
        )

    def aggregate(early, sources, chunk):
        return call(
            late_kernel,
            "aggregate",
            parts_of(blocks, size),
            3,
            made["index"],
            made["tiles"],
            made["inverse"],
            early,
            *sources,
            held=(pad - late, size, BLK),
            plan=plan,
            pad=pad,
            late=late,
            chunk=chunk,
        )

    def own_product(layer, full):
        return pl.pallas_call(
            functools.partial(self_kernel, feats=feat_size),
            name="own_product",
            in_specs=[VMEM] * 3,
            out_specs=VMEM,
            out_shape=pltpu.VMEM((blocks, cols, BLK), jnp.float32),
            compiler_params=params(),
            cost_estimate=cost(2),
        )(made["own"][layer], own_bias[layer], full)

    def update(weights, before, parts, low, kind):
        shapes = [pltpu.VMEM((blocks, cols, BLK), jnp.float32)]
        if kind != "sum":
            shapes = [parts_of(blocks, cols)]
        return pl.pallas_call(
            functools.partial(update_kernel, count=len(parts), low=low, kind=kind),
            name="update",
            in_specs=[VMEM] * (2 + len(parts)),
            out_specs=[VMEM] * len(shapes),
            out_shape=shapes,
            compiler_params=params(),
            cost_estimate=cost(3),
        )(weights, before, *parts)

    def send(x, pairs):
        return lax.ppermute(x, "dom", pairs)

    def from_line(hidden, layer, full):
        up = [(i, i + 2) for i in range(n - 2)]
        down = [(i + 2, i) for i in range(n - 2)]
        mix = [(0, 6), (1, 7), (6, 0), (7, 1), (2, 4), (3, 5), (4, 2), (5, 3)]
        outward = [(2, 0), (3, 1), (4, 6), (5, 7)]
        below, above = send(hidden, up), send(hidden, down)
        x_own = from_partner(pick(hidden, 0))
        below, above, x_own, _ = lax.optimization_barrier((below, above, x_own, made["index"]))
        shapes = [parts_of(slots, cols)] + [parts_of(blocks, size)] * (2 * chunks)
        x_near, *onwards = call(near_kernel, "near", shapes, 2, picks, hidden, below, above)
        degrees(x_near)
        x_near = from_partner(x_near)
        weights(x_near)
        far = [
            (send(onwards[2 * c], mix), send(onwards[2 * c + 1], outward)) for c in range(chunks)
        ]
        early = sum_early([hidden, below, above, x_own, x_near])
        state = own_product(layer, full)
        listed = []
        for c, (mixed, onward) in enumerate(far):
            mixed, onward = far[c] = tie((mixed, onward), early, state, listed)
            shape = parts_of(2 * slots, size)
            listed.append(
                call(far_kernel, "far", shape, 1, picks, above, mixed, onward, chunk=c)
            )
        aggs = []
        for c, (mixed, onward) in enumerate(far):
            x_far = from_partner(listed[c])
            x_far, *_ = tie((x_far,), listed, aggs)
            aggs.append(aggregate(early, [mixed, onward, x_far], c))
        return aggs, state

    def from_ring(hidden, layer, full):
        behind, ahead = from_behind(hidden, 2), from_behind(hidden, -2)
        behind_two, ahead_two = from_behind(behind, 2), from_behind(ahead, -2)
        x_own = from_partner(pick(hidden, 0))
        x_near = [from_partner(pick(behind, 1)), from_partner(pick(ahead, depth - 1))]
        degrees()
        weights()
        odd = me % 2 == 1
        x_two = jnp.where(odd, pick(behind_two, 2), pick(ahead_two, depth - 2))
        early = sum_early([hidden, behind, ahead, x_own, *x_near])
        aggs = [aggregate(early, [behind_two, ahead_two, from_partner(x_two)], 0)]
        return aggs, own_product(layer, full)

    for layer in range(layers):
        last = layer == layers - 1
        full = lax.all_gather(hidden, "feat", axis=0, tiled=True)
        aggs, state = from_line(hidden, layer, full) if line else from_ring(hidden, layer, full)
        for c, agg in enumerate(aggs):
            other = from_feat(agg, 2)
            parts = [agg, from_feat(agg, 1), other, from_feat(other, 1)]
            kind = "sum" if c < chunks - 1 else "none" if last else "relu"
            (state,) = update(made["nbr"][layer], state, parts, c * feat_size * size, kind)
        hidden = state
    return hidden.transpose(0, 2, 1).reshape(node_rows, cols)


def solution(mesh):
    in_specs = (
        P("dom", "feat"),
        P("dom", None, None),
        P("dom"),
        P("dom"),
        P("dom"),
        P("dom", None, None),
        P("dom", None),
        P(),
        P(),
        P(),
    )
    out_specs = P("dom", "feat")
    return jax.shard_map(
        per_device, mesh=mesh, in_specs=in_specs, out_specs=out_specs, check_vma=False
    )
```

```python
import functools

import jax
import jax.numpy as jnp
from jax import lax
from jax.experimental import pallas as pl
from jax.experimental.pallas import tpu as pltpu
from jax.sharding import PartitionSpec as P

BLK = 128
GROUP = 4
SIDE = 8
CHUNKS = 2
VMEM = pl.BlockSpec(memory_space=pltpu.VMEM)
SMEM = pl.BlockSpec(memory_space=pltpu.SMEM)


def params():
    return pltpu.CompilerParams(vmem_limit_bytes=18 * 2**20)


def cost(us):
    return pl.CostEstimate(
        flops=int(us * 1e9), bytes_accessed=int(us * 3e6), transcendentals=0
    )


def offset_of(d):
    return (d // 2 + 1) * (1 if d % 2 == 0 else -1)


def peer_of(offset):
    return 2 * (offset - 1) if offset > 0 else 2 * (-offset - 1) + 1


def peer_near(offset, n, peers=8):
    near = (offset + n // 2) % n - n // 2
    for d in range(peers):
        if offset_of(d) == near:
            return d
    return None


def from_behind(x, distance):
    n = lax.axis_size("dom")
    return lax.ppermute(x, "dom", [(i, (i + distance) % n) for i in range(n)])


def from_partner(x):
    n = lax.axis_size("dom")
    return lax.ppermute(x, "dom", [(i, i ^ 1) for i in range(n)])


def from_feat(x, bit):
    n = lax.axis_size("feat")
    return lax.ppermute(x, "feat", [(i, i ^ bit) for i in range(n)])


class Plan:
    def __init__(self, blocks, slots, tiles):
        self.blocks, self.slots = blocks, slots
        lists = 2 * blocks
        longest = tiles + lists * (GROUP - 1)
        self.longest = -(-longest // GROUP) * GROUP
        self.order_at = lists + 1
        self.srcs_at = self.order_at + self.longest
        self.size = self.srcs_at + self.longest

    def views(self, ref):
        return ref, Shifted(ref, self.order_at), Shifted(ref, self.srcs_at)


def picks_kernel(spot, mine, out):
    me = spot[0]
    odd = me % 2 == 1
    layers, _, width = mine.shape
    slots = width - 1
    for k in range(layers):
        peer_even = peer_near(1 + 2 * k, 2 * layers)
        peer_odd = peer_near(-1 + 2 * k, 2 * layers)
        for s in range(slots):
            even_one = 0 if peer_even is None else mine[k, peer_even, s]
            odd_one = 0 if peer_odd is None else mine[k, peer_odd, s]
            out[k, s] = jnp.where(odd, odd_one, even_one)
    low_end = me < 2
    for s in range(slots):
        up_from = jnp.where(odd, mine[0, peer_of(-3), s], mine[0, peer_of(-1), s])
        down_from = jnp.where(odd, mine[0, peer_of(1), s], mine[0, peer_of(3), s])
        out[layers, s] = jnp.where(low_end, up_from, down_from)
        out[layers + 1, s] = jnp.where(
            low_end, mine[0, peer_of(-2), s], mine[0, peer_of(2), s]
        )
        out[layers + 2, s] = me


class Shifted:
    def __init__(self, ref, at):
        self.ref, self.at = ref, at

    def __getitem__(self, i):
        return self.ref[self.at + i]

    def __setitem__(self, i, value):
        self.ref[self.at + i] = value


def plan_kernel(spot, count, dst, src, mine, theirs, out, place, cursor, *, bases, pad, late, plan):
    starts, order, srcs = plan.views(out)
    lists = 2 * plan.blocks
    blocks = plan.blocks
    me = spot[0]
    odd = me % 2 == 1
    layer_here = me // 2
    layers = mine.shape[0]
    peers, width = mine.shape[1:]
    slots = width - 1
    live = count[0]

    def own(b, _):
        place[b] = b
        return 0

    lax.fori_loop(0, blocks, own, 0)
    for d in range(peers):
        o = offset_of(d)
        if o % 2 == 0:
            k = (o // 2) % layers
            base, listed = bases(layer_here, k, False)

            def enter(s, _, d=d, k=k, base=base, listed=listed):
                at = base + jnp.where(listed, s, mine[k, d, s])
                place[blocks + d * slots + s] = jnp.where(s < mine[k, d, slots], at, pad - 1)
                return 0
        else:
            k = jnp.where(odd, ((o - 1) // 2) % layers, ((o + 1) // 2) % layers)
            base_even = bases(layer_here, ((o + 1) // 2) % layers, True)[0]
            base_odd = bases(layer_here, ((o - 1) // 2) % layers, True)[0]
            base = jnp.where(odd, base_odd, base_even)

            def enter(s, _, d=d, k=k, base=base):
                live_slot = s < theirs[k, d, slots]
                place[blocks + d * slots + s] = jnp.where(live_slot, base + s, pad - 1)
                return 0

        lax.fori_loop(0, slots, enter, 0)
    def clear(b, _):
        cursor[b] = 0
        return 0

    lax.fori_loop(0, lists, clear, 0)

    def list_of(t):
        at = place[src[t]]
        return dst[t] + jnp.where((at >= late) & (at < pad - 1), blocks, 0), at

    def tally(t, _):
        b, _at = list_of(t)
        cursor[b] = cursor[b] + 1
        return 0

    lax.fori_loop(0, live, tally, 0)

    def begin(b, at):
        starts[b] = at
        groups = (cursor[b] + GROUP - 1) // GROUP
        cursor[b] = at * GROUP
        return at + groups

    starts[lists] = lax.fori_loop(0, lists, begin, 0)

    def put(t, _):
        b, at = list_of(t)
        p = cursor[b]
        order[p] = t
        srcs[p] = at
        cursor[b] = p + 1
        return 0

    for p in range(GROUP):
        order[p] = 0
        srcs[p] = pad
    lax.fori_loop(0, live, put, 0)

    def fill_up(b, _):
        def fill(p, _):
            order[p] = 0
            srcs[p] = pad
            return 0

        lax.fori_loop(cursor[b], starts[b + 1] * GROUP, fill, 0)
        return 0

    lax.fori_loop(0, lists, fill_up, 0)


def side_by_side(starts, first, sums, product):
    lows = [starts[first + u] for u in range(SIDE)]
    highs = [starts[first + u + 1] for u in range(SIDE)]
    steps = functools.reduce(jnp.maximum, [h - l for h, l in zip(highs, lows)])

    def step(g, sums):
        out = []
        for u in range(SIDE):
            inside = lows[u] + g < highs[u]
            at = jnp.where(inside, lows[u] + g, 0) * GROUP
            out.append(sums[u] + product(at, inside))
        return tuple(out)

    return lax.fori_loop(0, steps, step, tuple(sums))


def zeros(rows):
    return [jnp.zeros((rows, BLK), jnp.float32) for _ in range(SIDE)]


def across(left, tiles, order, at):
    right = jnp.concatenate([tiles[order[at + k]] for k in range(GROUP)], axis=1)
    return lax.dot_general(
        left, right, (((1,), (1,)), ((), ())), preferred_element_type=jnp.float32
    )


def degree_kernel(index, tiles, inverse, kept, *, plan, pad):
    starts, order, srcs = plan.views(index)

    def keep(t, _):
        for k in range(4):
            kept[4 * t + k] = tiles[4 * t + k]
        return 0

    lax.fori_loop(0, tiles.shape[0] // 4, keep, 0, unroll=4)

    def product(at, inside):
        ones = [
            jnp.full(
                (8, BLK),
                jnp.where(inside & (srcs[at + k] != pad), 1.0, 0.0),
                jnp.float32,
            )
            for k in range(GROUP)
        ]
        left = jnp.concatenate(ones, axis=1).astype(jnp.bfloat16)
        return across(left, tiles, order, at)

    blocks = inverse.shape[0]
    for first in range(0, blocks, SIDE):
        sums = side_by_side(starts, first, zeros(8), product)
        sums = side_by_side(starts, blocks + first, sums, product)
        for u in range(SIDE):
            inverse[first + u] = 1.0 / (1.0 + sums[u])


def hold(held, refs):
    base = 0
    for ref in refs:

        def copy(i, _, ref=ref, base=base):
            for k in range(4):
                held[base + 4 * i + k] = ref[4 * i + k]
            return 0

        lax.fori_loop(0, ref.shape[0] // 4, copy, 0, unroll=True)
        base += ref.shape[0]
    held[base] = jnp.zeros(held.shape[1:], held.dtype)
    return base


def early_kernel(index, tiles, *rest, plan, pad):
    *sources, out, held = rest
    starts, order, srcs = plan.views(index)
    end = hold(held, sources)

    def product(at, inside):
        left = []
        for k in range(GROUP):
            src = jnp.where(inside, srcs[at + k], pad)
            left.append(held[jnp.minimum(src, end)])
        return across(jnp.concatenate(left, axis=1), tiles, order, at)

    for first in range(0, out.shape[0], SIDE):
        sums = side_by_side(starts, first, zeros(held.shape[1]), product)
        for u in range(SIDE):
            out[first + u] = sums[u]


def late_kernel(index, tiles, inverse, early, *rest, plan, pad, late, chunk):
    *sources, out, held = rest
    starts, order, srcs = plan.views(index)
    end = hold(held, sources)
    size = held.shape[1]
    cut = slice(chunk * size, (chunk + 1) * size)

    def product(at, inside):
        left = []
        for k in range(GROUP):
            src = jnp.where(inside, srcs[at + k], pad) - late
            left.append(held[jnp.clip(src, 0, end)])
        return across(jnp.concatenate(left, axis=1), tiles, order, at)

    blocks = out.shape[0]
    for first in range(0, blocks, SIDE):
        sums = [early[first + u, cut] for u in range(SIDE)]
        sums = side_by_side(starts, blocks + first, sums, product)
        for u in range(SIDE):
            out[first + u] = (sums[u] * inverse[first + u][:1]).astype(out.dtype)


def weights_kernel(spot, w, out, *, feats, chunks, relative):
    cols, width = out.shape
    here = spot[1]
    rows = []
    if relative:
        size = cols // chunks
        for c in range(chunks):
            for k in range(feats):
                at = pl.multiple_of((here ^ k) * cols + c * size, 16)
                rows.append(w[pl.ds(at, size), :])
        rows = jnp.concatenate(rows, axis=0)
    else:
        rows = w[...]
    column = lax.broadcasted_iota(jnp.int32, (cols, width), 1)
    wanted = lax.broadcasted_iota(jnp.int32, (cols, width), 0) + here * cols
    pick = jnp.where(column == wanted, 1.0, 0.0).astype(rows.dtype)
    turned = lax.dot_general(
        pick, rows, (((1,), (1,)), ((), ())), preferred_element_type=jnp.float32
    )
    out[...] = turned.astype(out.dtype)


def pick_kernel(picks, source, out, *, row):
    def copy(s, _):
        out[s] = source[picks[row, s]]
        return 0

    lax.fori_loop(0, out.shape[0], copy, 0, unroll=True)


def near_kernel(picks, own, below, above, x_out, *outs):
    layer_here = picks[picks.shape[0] - 1, 0] // 2
    slots, blocks = x_out.shape[0], own.shape[0]
    mixed, onward = outs[0::2], outs[1::2]
    size = mixed[0].shape[1]
    cuts = [slice(c * size, (c + 1) * size) for c in range(len(mixed))]

    def copy(s, _):
        x_out[s] = jnp.where(layer_here == 0, above[picks[3, s]], below[picks[1, s]])
        return 0

    lax.fori_loop(0, slots, copy, 0, unroll=True)

    @pl.when((layer_here == 0) | (layer_here == 3))
    def _():
        def copy(s, _):
            for c, cut in enumerate(cuts):
                mixed[c][s] = own[picks[4, s], cut]
                mixed[c][slots + s] = own[picks[5, s], cut]
            return 0

        lax.fori_loop(0, slots, copy, 0, unroll=True)

    def relay(through, back):
        def copy(i, _):
            for k in range(2):
                for c, cut in enumerate(cuts):
                    mixed[c][2 * i + k] = through[2 * i + k, cut]
                    onward[c][2 * i + k] = back[2 * i + k, cut]
            return 0

        lax.fori_loop(0, blocks // 2, copy, 0, unroll=True)

    @pl.when(layer_here == 1)
    def _():
        relay(below, above)

    @pl.when(layer_here == 2)
    def _():
        relay(above, below)


def far_kernel(picks, above, mixed, onward, out, *, chunk):
    layer_here = picks[picks.shape[0] - 1, 0] // 2
    slots, size = picks.shape[1], mixed.shape[1]
    cut = slice(chunk * size, (chunk + 1) * size)
    end = (layer_here == 0) | (layer_here == 3)

    @pl.when(end)
    def _():
        def copy(s, _):
            out[s] = onward[picks[2, s]]
            out[slots + s] = mixed[s]
            return 0

        lax.fori_loop(0, slots, copy, 0, unroll=True)

    @pl.when(jnp.logical_not(end))
    def _():
        def copy(s, _):
            out[s] = above[picks[3, s], cut]
            out[slots + s] = mixed[picks[2, s]]
            return 0

        lax.fori_loop(0, slots, copy, 0, unroll=True)


def pair_of(ref, b):
    return jnp.concatenate([ref[b], ref[b + 1]], axis=1)


def self_kernel(weights, bias, full, out, *, feats):
    blocks = out.shape[0]

    def body(q, _):
        parts = [pair_of(full, f * blocks + 2 * q) for f in range(feats)]
        sums = lax.dot_general(
            weights[...],
            jnp.concatenate(parts, axis=0),
            (((1,), (0,)), ((), ())),
            preferred_element_type=jnp.float32,
        )
        sums = sums + bias[...]
        out[2 * q] = sums[:, :BLK]
        out[2 * q + 1] = sums[:, BLK:]
        return 0

    lax.fori_loop(0, blocks // 2, body, 0, unroll=True)


def update_kernel(weights, before, *rest, count, low, kind):
    parts, out = rest[:count], rest[count]
    blocks = out.shape[0]

    def body(q, _):
        rows = jnp.concatenate([pair_of(ref, 2 * q) for ref in parts], axis=0)
        sums = lax.dot_general(
            weights[:, low : low + rows.shape[0]],
            rows,
            (((1,), (0,)), ((), ())),
            preferred_element_type=jnp.float32,
        )
        for k in range(2):
            pre = sums[:, k * BLK : (k + 1) * BLK] + before[2 * q + k]
            if kind == "relu":
                pre = jnp.maximum(pre, 0.0)
            out[2 * q + k] = pre.astype(out.dtype)
        return 0

    lax.fori_loop(0, blocks // 2, body, 0, unroll=True)


def tie(first, *others):
    return lax.optimization_barrier((tuple(first), *others))[0]


def line_base(blocks, slots):
    late = 3 * blocks + 2 * slots
    mixed, onward, x_far = late, late + blocks, late + 2 * blocks

    def base(layer_here, k, partner):
        middle = (layer_here == 1) | (layer_here == 2)
        lacking = layer_here == (0 if k == 1 else 3)
        if not partner:
            if k == 2:
                return jnp.where(middle, mixed, onward), False
            return jnp.where(lacking, mixed + slots, blocks + k // 2 * blocks), lacking
        if k == 0:
            return 3 * blocks, True
        if k == 2:
            return jnp.where(middle, x_far + slots, x_far), True
        here = 3 * blocks + slots
        if k == 3:
            here = jnp.where(layer_here == 0, here, x_far)
        return jnp.where(lacking, x_far + slots, here), True

    return base


def ring_base(blocks, slots, layers):
    def base(layer_here, k, partner):
        del layer_here
        if partner:
            if k in (2, layers - 2):
                return 5 * blocks + 3 * slots, True
            return 3 * blocks + {0: 0, 1: 1, layers - 1: 2}[k] * slots, True
        if k in (2, layers - 2):
            return 3 * blocks + 3 * slots + (0 if k == 2 else blocks), False
        return {1: 1, layers - 1: 2}[k] * blocks, False

    return base


def per_device(
    feats, tile_vals, tile_dst, tile_src, tile_count, send_blocks, send_count, w_self, w_nbr, bias
):
    n = lax.axis_size("dom")
    feat_size = lax.axis_size("feat")
    me = lax.axis_index("dom")
    feat_here = lax.axis_index("feat")
    node_rows, cols = feats.shape
    blocks = node_rows // BLK
    tiles_here = tile_vals.shape[0]
    peers, slots = send_blocks.shape[1:]
    layers, width = bias.shape
    depth = n // 2
    line = depth == 4
    chunks = CHUNKS if line else 1
    size = cols // chunks
    spot = jnp.stack([me, feat_here]).astype(jnp.int32)
    plan = Plan(blocks, slots, tiles_here)

    own_table = jnp.concatenate([send_blocks, send_count[:, :, None]], axis=2)
    near_by = {1: 2, 2: 4, depth - 2: -4, depth - 1: -2}
    far_tables = [
        from_behind(own_table, near_by[k]) if k in near_by else own_table for k in range(1, depth)
    ]
    mine = jnp.concatenate([own_table, *far_tables], axis=0)
    theirs = from_partner(mine)

    hidden = feats.reshape(blocks, BLK, cols).transpose(0, 2, 1)

    if line:
        late, pad = 3 * blocks + 2 * slots, 5 * blocks + 4 * slots + 1
        bases = line_base(blocks, slots)
    else:
        late, pad = 3 * blocks + 3 * slots, 5 * blocks + 4 * slots + 1
        bases = ring_base(blocks, slots, depth)

    picks = pl.pallas_call(
        picks_kernel,
        name="picks",
        in_specs=[SMEM] * 2,
        out_specs=SMEM,
        out_shape=jax.ShapeDtypeStruct((depth + 3, slots), jnp.int32),
        cost_estimate=cost(1),
    )(spot, mine)
    def call(kernel, name, out_shape, us, scalars, *args, held=None, **static):
        return pl.pallas_call(
            functools.partial(kernel, **static),
            name=name,
            in_specs=[SMEM] + [VMEM] * len(args),
            out_specs=jax.tree.map(lambda _: VMEM, out_shape),
            out_shape=out_shape,
            scratch_shapes=[] if held is None else [pltpu.VMEM(held, jnp.bfloat16)],
            compiler_params=params(),
            cost_estimate=cost(us),
        )(scalars, *args)

    made = {}

    made["index"] = pl.pallas_call(
        functools.partial(plan_kernel, bases=bases, pad=pad, late=late, plan=plan),
        name="plan",
        in_specs=[SMEM] * 6,
        out_specs=SMEM,
        out_shape=jax.ShapeDtypeStruct((plan.size,), jnp.int32),
        scratch_shapes=[
            pltpu.SMEM((blocks + peers * slots,), jnp.int32),
            pltpu.SMEM((2 * blocks,), jnp.int32),
        ],
        cost_estimate=cost(5),
    )(spot, tile_count, tile_dst, tile_src, mine, theirs)

    def degrees(*after):
        if "tiles" in made:
            return
        (tiles_in,) = tie((tile_vals,), *after)
        made["inverse"], made["tiles"] = call(
            degree_kernel,
            "degree",
            [
                pltpu.VMEM((blocks, 8, BLK), jnp.float32),
                pltpu.VMEM(tile_vals.shape, tile_vals.dtype),
            ],
            0.01,
            made["index"],
            tiles_in,
            plan=plan,
            pad=pad,
        )

    def turned_weights(w, relative):
        return pl.pallas_call(
            functools.partial(
                weights_kernel, feats=feat_size, chunks=chunks, relative=relative
            ),
            name="turn_weights",
            grid=(layers,),
            in_specs=[SMEM, pl.BlockSpec((None, width, width), lambda l: (l, 0, 0))],
            out_specs=pl.BlockSpec((None, cols, width), lambda l: (l, 0, 0)),
            out_shape=jax.ShapeDtypeStruct((layers, cols, width), w.dtype),
            compiler_params=params(),
            cost_estimate=cost(0.01),
        )(spot, w)

    own_bias = lax.dynamic_slice_in_dim(bias, feat_here * cols, cols, 1)[:, :, None]

    def weights(*after):
        if "own" not in made:
            made["own"] = turned_weights(tie((w_self,), *after)[0], False)
            made["nbr"] = turned_weights(tie((w_nbr,), *after)[0], True)

    def parts_of(number, rows):
        return jax.ShapeDtypeStruct((number, rows, BLK), jnp.bfloat16)

    def pick(source, row):
        return call(pick_kernel, "pick", parts_of(slots, cols), 1, picks, source, row=row)

    def sum_early(sources):
        return call(
            early_kernel,
            "sum_early",
            pltpu.VMEM((blocks, cols, BLK), jnp.float32),
            6,
            made["index"],
            made["tiles"],
            *sources,
            held=(late + 1, cols, BLK),
            plan=plan,
            pad=pad,
        )

    def aggregate(early, sources, chunk):
        return call(
            late_kernel,
            "aggregate",
            parts_of(blocks, size),
            3,
            made["index"],
            made["tiles"],
            made["inverse"],
            early,
            *sources,
            held=(pad - late, size, BLK),
            plan=plan,
            pad=pad,
            late=late,
            chunk=chunk,
        )

    def own_product(layer, full):
        return pl.pallas_call(
            functools.partial(self_kernel, feats=feat_size),
            name="own_product",
            in_specs=[VMEM] * 3,
            out_specs=VMEM,
            out_shape=pltpu.VMEM((blocks, cols, BLK), jnp.float32),
            compiler_params=params(),
            cost_estimate=cost(2),
        )(made["own"][layer], own_bias[layer], full)

    def update(weights, before, parts, low, kind):
        shapes = [pltpu.VMEM((blocks, cols, BLK), jnp.float32)]
        if kind != "sum":
            shapes = [parts_of(blocks, cols)]
        return pl.pallas_call(
            functools.partial(update_kernel, count=len(parts), low=low, kind=kind),
            name="update",
            in_specs=[VMEM] * (2 + len(parts)),
            out_specs=[VMEM] * len(shapes),
            out_shape=shapes,
            compiler_params=params(),
            cost_estimate=cost(3),
        )(weights, before, *parts)

    def send(x, pairs):
        return lax.ppermute(x, "dom", pairs)

    def from_line(hidden, layer, full):
        up = [(i, i + 2) for i in range(n - 2)]
        down = [(i + 2, i) for i in range(n - 2)]
        mix = [(0, 6), (1, 7), (6, 0), (7, 1), (2, 4), (3, 5), (4, 2), (5, 3)]
        outward = [(2, 0), (3, 1), (4, 6), (5, 7)]
        below, above = send(hidden, up), send(hidden, down)
        x_own = from_partner(pick(hidden, 0))
        below, above, x_own, _ = lax.optimization_barrier((below, above, x_own, made["index"]))
        shapes = [parts_of(slots, cols)] + [parts_of(blocks, size)] * (2 * chunks)
        x_near, *onwards = call(near_kernel, "near", shapes, 2, picks, hidden, below, above)
        degrees(x_near)
        x_near = from_partner(x_near)
        weights(x_near)
        far = [
            (send(onwards[2 * c], mix), send(onwards[2 * c + 1], outward)) for c in range(chunks)
        ]
        early = sum_early([hidden, below, above, x_own, x_near])
        state = own_product(layer, full)
        listed = []
        for c, (mixed, onward) in enumerate(far):
            mixed, onward = far[c] = tie((mixed, onward), early, state, listed)
            shape = parts_of(2 * slots, size)
            listed.append(
                call(far_kernel, "far", shape, 1, picks, above, mixed, onward, chunk=c)
            )
        aggs = []
        for c, (mixed, onward) in enumerate(far):
            x_far = from_partner(listed[c])
            x_far, *_ = tie((x_far,), listed, aggs)
            aggs.append(aggregate(early, [mixed, onward, x_far], c))
        return aggs, state

    def from_ring(hidden, layer, full):
        behind, ahead = from_behind(hidden, 2), from_behind(hidden, -2)
        behind_two, ahead_two = from_behind(behind, 2), from_behind(ahead, -2)
        x_own = from_partner(pick(hidden, 0))
        x_near = [from_partner(pick(behind, 1)), from_partner(pick(ahead, depth - 1))]
        degrees()
        weights()
        odd = me % 2 == 1
        x_two = jnp.where(odd, pick(behind_two, 2), pick(ahead_two, depth - 2))
        early = sum_early([hidden, behind, ahead, x_own, *x_near])
        aggs = [aggregate(early, [behind_two, ahead_two, from_partner(x_two)], 0)]
        return aggs, own_product(layer, full)

    for layer in range(layers):
        last = layer == layers - 1
        full = lax.all_gather(hidden, "feat", axis=0, tiled=True)
        aggs, state = from_line(hidden, layer, full) if line else from_ring(hidden, layer, full)
        for c, agg in enumerate(aggs):
            other = from_feat(agg, 2)
            parts = [agg, from_feat(agg, 1), other, from_feat(other, 1)]
            kind = "sum" if c < chunks - 1 else "none" if last else "relu"
            (state,) = update(made["nbr"][layer], state, parts, c * feat_size * size, kind)
        hidden = state
    return hidden.transpose(0, 2, 1).reshape(node_rows, cols)


def solution(mesh):
    in_specs = (
        P("dom", "feat"),
        P("dom", None, None),
        P("dom"),
        P("dom"),
        P("dom"),
        P("dom", None, None),
        P("dom", None),
        P(),
        P(),
        P(),
    )
    out_specs = P("dom", "feat")
    return jax.shard_map(
        per_device, mesh=mesh, in_specs=in_specs, out_specs=out_specs, check_vma=False
    )
```
